32 devices in a mesh: row: 4 (over x, core), col: 8 (over z, y).
Axes of the slice: x: 2, y: 2, z: 4, core: 2. Of those that a mesh axis runs over, the one named last changes fastest.
Arguments:
- tokens: bfloat16 [128, 8192], P('col', 'row'), may hold values from -6 to 6
- cotangent: bfloat16 [128, 8192], P('col', 'row'), may hold values from -1.5 to 1.5
- gate_weight: bfloat16 [8192, 14336], P('row', 'col'), may hold values from -0.0625 to 0.0625
- up_weight: bfloat16 [8192, 14336], P('row', 'col'), may hold values from -0.0625 to 0.0625
- down_weight: bfloat16 [14336, 8192], P('col', 'row'), may hold values from -0.046875 to 0.046875
Outputs:
- grad_tokens: bfloat16 [128, 8192], P('col', 'row')
- grad_gate: bfloat16 [8192, 14336], P('row', 'col')
- grad_up: bfloat16 [8192, 14336], P('row', 'col')
- grad_down: bfloat16 [14336, 8192], P('col', 'row')
The draws below stay inside these ranges and needn't reach their ends.
All inputs are finite; a program needn't handle non-finite values.
Results may differ from the reference program's by a relative error of at most 0.0051.
Values may be sent and summed in bfloat16 or wider, within the bound.
A program may use at most 128 MiB of HBM per device.

```python
import jax
import jax.numpy as jnp
from jax import lax

D = 8192
FF = 14336
TOKENS = 128


def block_scale(stream_key, extent, cuts, least, high):
    level, own = 1.0, jax.random.fold_in(stream_key, 6)
    for position, parts in cuts:
        steps = jnp.exp(jax.random.uniform(jax.random.fold_in(own, position), (parts,), jnp.float32, least / len(cuts), high / len(cuts)))
        level = level * jnp.repeat(steps, extent[position] // parts).reshape([-1 if axis == position else 1 for axis in range(len(extent))])
    return level


def noise(stream_key, dims, scale, reach, shards=(), kind=jnp.bfloat16):
    loudness = block_scale(stream_key, dims, shards, -0.22, 0.18) if shards else 1.0
    entries = jax.random.normal(stream_key, dims, jnp.float32) * scale * loudness
    return jnp.minimum(jnp.maximum(entries, -reach), reach).astype(kind)


def setup_inputs(seed: int = 0) -> dict:
    key_of = jax.random.split(jax.random.key(seed), 6)
    return {
        "tokens": noise(key_of[0], (TOKENS, D), 1.0, 6.0, ((0, 8), (1, 4))),
        "cotangent": noise(key_of[1], (TOKENS, D), 0.25, 1.5, ((0, 8), (1, 4))),
        "gate_weight": noise(key_of[2], (D, FF), D ** -0.5, 0.0625, ((0, 4), (1, 8))),
        "up_weight": noise(key_of[3], (D, FF), D ** -0.5, 0.0625, ((0, 4), (1, 8))),
        "down_weight": noise(key_of[4], (FF, D), FF ** -0.5, 0.046875, ((0, 8), (1, 4))),
    }


def contract_last(left, right):
    return lax.dot_general(left, right, (((1,), (1,)), ((), ())), preferred_element_type=jnp.float32)


def contract_first(left, right):
    return lax.dot_general(left, right, (((0,), (0,)), ((), ())), preferred_element_type=jnp.float32)


def reference(tokens, cotangent, gate_weight, up_weight, down_weight):
    gate = jnp.dot(tokens, gate_weight, preferred_element_type=jnp.float32)
    up = jnp.dot(tokens, up_weight, preferred_element_type=jnp.float32)
    sig = jax.nn.sigmoid(gate)
    act = gate * sig
    hidden = (act * up).astype(jnp.bfloat16)
    grad_hidden = contract_last(cotangent, down_weight)
    d_up = (grad_hidden * act).astype(jnp.bfloat16)
    d_gate = (grad_hidden * up * sig * (1.0 + gate * (1.0 - sig))).astype(jnp.bfloat16)
    grad_tokens = (contract_last(d_gate, gate_weight) + contract_last(d_up, up_weight)).astype(jnp.bfloat16)
    grad_gate = contract_first(tokens, d_gate).astype(jnp.bfloat16)
    grad_up = contract_first(tokens, d_up).astype(jnp.bfloat16)
    grad_down = contract_first(hidden, cotangent).astype(jnp.bfloat16)
    return grad_tokens, grad_gate, grad_up, grad_down
```

```python
import functools

import jax
import jax.numpy as jnp
from jax import lax
from jax.experimental import pallas as pl
from jax.experimental.pallas import tpu as pltpu
from jax.sharding import PartitionSpec as P

MESH = pl.DeviceIdType.MESH
F32, BF16 = jnp.float32, jnp.bfloat16
TILE = 256
GROUPS = 4


def contract_last(left, right):
    return lax.dot_general(
        left, right, (((1,), (1,)), ((), ())), preferred_element_type=F32
    )


def contract_first(left, right):
    return lax.dot_general(
        left, right, (((0,), (0,)), ((), ())), preferred_element_type=F32
    )


def main_kernel(
    tok_ref, cot_ref, wg_hbm, wu_hbm, wd_hbm,
    gt_ref, tok_out, cot_out, dg_out, du_out, hid_out,
    tok_all, cot_all, wg, wu, wd,
    own, core_send, core_recv, x_send, x_recv,
    dg, du, hid,
    part, y_send, y_recv, z_send, z_recv, mine,
    w_sem, out_sem, a_send, a_recv, c_ssem, c_rsem, x_ssem, x_rsem,
    h_ssem, h_rsem, y_ssem, y_rsem, z_ssem, z_rsem,
):
    row, col = lax.axis_index("row"), lax.axis_index("col")
    core, zy = lax.rem(row, 2), lax.rem(col, 2)
    sib = row + 1 - 2 * core
    across = lax.rem(row + 2, 4)
    y_peer = col + 1 - 2 * zy
    z = col // 2
    z_to = [None] + [lax.rem(col + 2 * d, 8) for d in (1, 2, 3)]
    z_from = [None] + [lax.rem(col + 8 - 2 * d, 8) for d in (1, 2, 3)]
    y_from = [None] + [lax.rem(y_peer + 8 - 2 * d, 8) for d in (1, 2, 3)]

    w_copies = [
        pltpu.make_async_copy(src, dst, w_sem.at[k])
        for k, (src, dst) in enumerate(((wg_hbm, wg), (wu_hbm, wu), (wd_hbm, wd)))
    ]
    for copy in w_copies:
        copy.start()

    barrier = pltpu.get_barrier_semaphore()
    for peer in ((sib, col), (across, col), (row, y_peer),
                 (row, z_to[1]), (row, z_to[2]), (row, z_to[3])):
        pl.semaphore_signal(barrier, inc=1, device_id=peer, device_id_type=MESH)
    pl.semaphore_wait(barrier, 6)

    def send(src, dst, ssem, rsem, peer):
        return pltpu.make_async_remote_copy(
            src_ref=src, dst_ref=dst, send_sem=ssem, recv_sem=rsem,
            device_id=peer, device_id_type=MESH,
        )

    n = tok_ref.shape[0]

    def block(index):
        return pl.ds(pl.multiple_of(index * n, n), n)

    gathers = ((tok_ref, tok_all), (cot_ref, cot_all))
    sends = []
    for a, (src, dst) in enumerate(gathers):
        for k, peer in ((2, z_to[2]), (1, z_to[1]), (3, z_to[3]), (0, y_peer)):
            sends.append(send(src, dst.at[block(col)], a_send.at[a, k], a_recv.at[a, k], (row, peer)))
            sends[-1].start()

    def arrived(a, k, source):
        dst = gathers[a][1].at[block(source)]
        send(dst, dst, a_send.at[a, k], a_recv.at[a, k], (row, y_peer)).wait_recv()

    def gather(a):
        src, dst = gathers[a]
        dst[block(col), :] = src[...]
        for d in (1, 3, 2):
            arrived(a, d, z_from[d])
            there = dst.at[block(z_from[d])]
            sends.append(send(there, there, a_send.at[a, 3 + d], a_recv.at[a, 3 + d], (row, y_peer)))
            sends[-1].start()
        arrived(a, 0, y_peer)
        for d in (1, 3, 2):
            arrived(a, 3 + d, y_from[d])

    width = wg.shape[1]
    half = tok_all.shape[0] // 2
    mine_rows = pl.ds(pl.multiple_of(core * half, half), half)

    def split(m, at, full):
        low, high = full[:half], full[half:]
        first = core == 0
        own[m, :, at] = jnp.where(first, low, high)
        core_send[m, :, at] = jnp.where(first, high, low)

    def forward(m):
        @pl.loop(0, width // TILE)
        def _(t):
            at = pl.ds(pl.multiple_of(t * TILE, TILE), TILE)
            if m == 2:
                full = contract_last(cot_all[...], wd[at, :])
            else:
                full = jnp.dot(tok_all[...], (wg, wu)[m][:, at], preferred_element_type=F32)
            split(m, at, full)

    c_copies = [send(core_send.at[m], core_recv.at[m], c_ssem.at[m], c_rsem.at[m], (sib, col)) for m in range(3)]
    x_copies = [send(x_send.at[m], x_recv.at[m], x_ssem.at[m], x_rsem.at[m], (across, col)) for m in range(3)]

    def over_chip(m):
        c_copies[m].wait_recv()

        @pl.loop(0, width // TILE)
        def _(t):
            at = pl.ds(pl.multiple_of(t * TILE, TILE), TILE)
            total = own[m, :, at] + core_recv[m, :, at]
            own[m, :, at] = total
            x_send[m, :, at] = total.astype(BF16)
        x_copies[m].start()

    gather(0)
    for m in range(3):
        if m == 2:
            gather(1)
        w_copies[m].wait()
        forward(m)
        c_copies[m].start()
        if m > 0:
            over_chip(m - 1)
    over_chip(2)

    outs = [
        pltpu.make_async_copy(src, dst, out_sem.at[k])
        for k, (src, dst) in enumerate(
            ((tok_all, tok_out), (cot_all, cot_out), (dg, dg_out), (du, du_out), (hid, hid_out)))
    ]
    outs[0].start()
    outs[1].start()

    for m in range(3):
        x_copies[m].wait_recv()

    @pl.loop(0, width // TILE)
    def _(t):
        at = pl.ds(pl.multiple_of(t * TILE, TILE), TILE)
        gate, up, grad_hidden = (own[m, :, at] + x_recv[m, :, at].astype(F32) for m in range(3))
        sig = jax.nn.sigmoid(gate)
        act = gate * sig
        hid[mine_rows, at] = (act * up).astype(BF16)
        du[mine_rows, at] = (grad_hidden * act).astype(BF16)
        dg[mine_rows, at] = (grad_hidden * up * sig * (1.0 + gate * (1.0 - sig))).astype(BF16)

    h_copies = [
        send(ref.at[mine_rows], ref.at[mine_rows], h_ssem.at[k], h_rsem.at[k], (sib, col))
        for k, ref in enumerate((dg, du, hid))
    ]
    for copy in h_copies:
        copy.start()
    their_rows = pl.ds(pl.multiple_of((1 - core) * half, half), half)
    for k, ref in enumerate((dg, du, hid)):
        there = ref.at[their_rows]
        send(there, there, h_ssem.at[k], h_rsem.at[k], (sib, col)).wait_recv()
    for k in (2, 3, 4):
        outs[k].start()

    span = wg.shape[0] // GROUPS
    y_copies = [send(y_send.at[g], y_recv.at[g], y_ssem.at[g], y_rsem.at[g], (row, y_peer)) for g in range(GROUPS)]
    z_copies = [
        [send(z_send.at[g, d - 1], z_recv.at[g, d - 1], z_ssem.at[g, d - 1], z_rsem.at[g, d - 1], (row, z_to[d]))
         for d in (1, 2, 3)]
        for g in range(GROUPS)
    ]

    def backward(g):
        @pl.loop(0, span // TILE)
        def _(t):
            at = pl.ds(pl.multiple_of(t * TILE, TILE), TILE)
            rows = pl.ds(pl.multiple_of(g * span + t * TILE, TILE), TILE)
            full = contract_last(dg[...], wg[rows, :]) + contract_last(du[...], wu[rows, :])
            part[g, :, :, at] = full.reshape(8, n, TILE)
        for k in range(4):
            y_send[g, k] = part[g, y_peer - 2 * z + 2 * k].astype(BF16)
        y_copies[g].start()

    def along_z(g):
        y_copies[g].wait_recv()
        for d in (1, 2, 3):
            to = lax.rem(z + d, 4)
            z_send[g, d - 1] = (part[g, 2 * to + zy] + y_recv[g, to].astype(F32)).astype(BF16)
            z_copies[g][d - 1].start()
        mine[g] = part[g, col] + y_recv[g, z].astype(F32)

    for g in range(GROUPS):
        backward(g)
        if g > 0:
            along_z(g - 1)
    along_z(GROUPS - 1)
    for g in range(GROUPS):
        total = mine[g]
        for d in (1, 2, 3):
            z_copies[g][d - 1].wait_recv()
            total = total + z_recv[g, d - 1].astype(F32)
        gt_ref[:, g * span:(g + 1) * span] = total.astype(BF16)

    for copy in sends + c_copies + x_copies + h_copies + y_copies:
        copy.wait_send()
    for group in z_copies:
        for copy in group:
            copy.wait_send()
    for copy in outs:
        copy.wait()


def main(tokens, cotangent, gate_weight, up_weight, down_weight):
    n, depth = tokens.shape
    width = gate_weight.shape[1]
    all_tokens = 8 * n
    half = all_tokens // 2
    span = depth // GROUPS
    hbm, vmem = pl.BlockSpec(memory_space=pl.ANY), pl.BlockSpec(memory_space=pltpu.VMEM)
    dma = pltpu.SemaphoreType.DMA
    return pl.pallas_call(
        main_kernel,
        out_shape=(
            jax.ShapeDtypeStruct((n, depth), BF16),
            jax.ShapeDtypeStruct((all_tokens, depth), BF16),
            jax.ShapeDtypeStruct((all_tokens, depth), BF16),
            jax.ShapeDtypeStruct((all_tokens, width), BF16),
            jax.ShapeDtypeStruct((all_tokens, width), BF16),
            jax.ShapeDtypeStruct((all_tokens, width), BF16),
        ),
        in_specs=[vmem, vmem, hbm, hbm, hbm],
        out_specs=(vmem, hbm, hbm, hbm, hbm, hbm),
        scratch_shapes=[
            pltpu.VMEM((all_tokens, depth), BF16),
            pltpu.VMEM((all_tokens, depth), BF16),
            pltpu.VMEM((depth, width), BF16),
            pltpu.VMEM((depth, width), BF16),
            pltpu.VMEM((width, depth), BF16),
            pltpu.VMEM((3, half, width), F32),
            pltpu.VMEM((3, half, width), F32),
            pltpu.VMEM((3, half, width), F32),
            pltpu.VMEM((3, half, width), BF16),
            pltpu.VMEM((3, half, width), BF16),
            pltpu.VMEM((all_tokens, width), BF16),
            pltpu.VMEM((all_tokens, width), BF16),
            pltpu.VMEM((all_tokens, width), BF16),
            pltpu.VMEM((GROUPS, 8, n, span), F32),
            pltpu.VMEM((GROUPS, 4, n, span), BF16),
            pltpu.VMEM((GROUPS, 4, n, span), BF16),
            pltpu.VMEM((GROUPS, 3, n, span), BF16),
            pltpu.VMEM((GROUPS, 3, n, span), BF16),
            pltpu.VMEM((GROUPS, n, span), F32),
            dma((3,)), dma((5,)), dma((2, 7)), dma((2, 7)),
            dma((3,)), dma((3,)), dma((3,)), dma((3,)),
            dma((3,)), dma((3,)), dma((GROUPS,)), dma((GROUPS,)),
            dma((GROUPS, 3)), dma((GROUPS, 3)),
        ],
        compiler_params=pltpu.CompilerParams(
            collective_id=0, has_side_effects=True, vmem_limit_bytes=56 * 1024 * 1024
        ),
    )(tokens, cotangent, gate_weight, up_weight, down_weight)


def weight_kernel(last, tok_ref, dg_ref, du_ref, hid_ref, cot_ref, gg_ref, gu_ref, gd_ref):
    tok = tok_ref[...]
    gg_ref[...] = contract_first(tok, dg_ref[...]).astype(BF16)
    gu_ref[...] = contract_first(tok, du_ref[...]).astype(BF16)

    @pl.when(pl.program_id(0) <= last)
    def _():
        gd_ref[...] = contract_first(hid_ref[...], cot_ref[...]).astype(BF16)


def weight_grads(tok_all, dg, du, hid, cot_all):
    rows, depth = tok_all.shape
    width = dg.shape[1]
    last = width // TILE - 1

    def whole(array):
        return pl.BlockSpec(array.shape, lambda i: (0, 0))

    return pl.pallas_call(
        functools.partial(weight_kernel, last),
        grid=(depth // TILE,),
        out_shape=(
            jax.ShapeDtypeStruct((depth, width), BF16),
            jax.ShapeDtypeStruct((depth, width), BF16),
            jax.ShapeDtypeStruct((width, depth), BF16),
        ),
        in_specs=[
            pl.BlockSpec((rows, TILE), lambda i: (0, i)),
            whole(dg),
            whole(du),
            pl.BlockSpec((rows, TILE), lambda i: (0, jnp.minimum(i, last))),
            whole(cot_all),
        ],
        out_specs=(
            pl.BlockSpec((TILE, width), lambda i: (i, 0)),
            pl.BlockSpec((TILE, width), lambda i: (i, 0)),
            pl.BlockSpec((TILE, depth), lambda i: (jnp.minimum(i, last), 0)),
        ),
        compiler_params=pltpu.CompilerParams(vmem_limit_bytes=40 * 1024 * 1024),
    )(tok_all, dg, du, hid, cot_all)


def local(tokens, cotangent, gate_weight, up_weight, down_weight):
    grad_tokens, tok_all, cot_all, dg, du, hid = main(
        tokens, cotangent, gate_weight, up_weight, down_weight
    )
    grad_gate, grad_up, grad_down = weight_grads(tok_all, dg, du, hid, cot_all)
    return (grad_tokens, grad_gate, grad_up, grad_down)


def gating(gate, up, grad_hidden):
    sig = jax.nn.sigmoid(gate)
    act = gate * sig
    hidden = (act * up).astype(BF16)
    d_up = (grad_hidden * act).astype(BF16)
    d_gate = (grad_hidden * up * sig * (1.0 + gate * (1.0 - sig))).astype(BF16)
    return d_gate, d_up, hidden


def local_any(tokens, cotangent, gate_weight, up_weight, down_weight):
    def gather(array, axis):
        return lax.all_gather(array, axis, axis=0, tiled=True)

    def scatter(array, axis):
        return lax.psum_scatter(array, axis, scatter_dimension=0, tiled=True)

    tok_all, cot_all = gather(tokens, "col"), gather(cotangent, "col")
    gate = scatter(jnp.dot(tok_all, gate_weight, preferred_element_type=F32), "row")
    up = scatter(jnp.dot(tok_all, up_weight, preferred_element_type=F32), "row")
    grad_hidden = scatter(contract_last(cot_all, down_weight), "row")
    dg, du, hid = (gather(part, "row") for part in gating(gate, up, grad_hidden))
    grad_tokens = scatter(
        contract_last(dg, gate_weight) + contract_last(du, up_weight), "col"
    ).astype(BF16)
    return (
        grad_tokens,
        contract_first(tok_all, dg).astype(BF16),
        contract_first(tok_all, du).astype(BF16),
        contract_first(hid, cot_all).astype(BF16),
    )


def solution(mesh):
    fits = mesh.shape["row"] == 4 and mesh.shape["col"] == 8
    return jax.shard_map(
        local if fits else local_any,
        mesh=mesh,
        in_specs=(
            P("col", "row"),
            P("col", "row"),
            P("row", "col"),
            P("row", "col"),
            P("col", "row"),
        ),
        out_specs=(P("col", "row"), P("row", "col"), P("row", "col"), P("col", "row")),
        check_vma=False,
    )
```

```python
import functools

import jax
import jax.numpy as jnp
from jax import lax
from jax.experimental import pallas as pl
from jax.experimental.pallas import tpu as pltpu
from jax.sharding import PartitionSpec as P

MESH = pl.DeviceIdType.MESH
F32, BF16 = jnp.float32, jnp.bfloat16
TILE = 256
GROUPS = 4
RELAY = 1


def contract_last(left, right):
    return lax.dot_general(
        left, right, (((1,), (1,)), ((), ())), preferred_element_type=F32
    )


def contract_first(left, right):
    return lax.dot_general(
        left, right, (((0,), (0,)), ((), ())), preferred_element_type=F32
    )


def main_kernel(
    tok_ref, cot_ref, wg_hbm, wu_hbm, wd_hbm,
    gt_ref, tok_out, cot_out, dg_out, du_out, hid_out,
    tok_all, cot_all, wg, wu, wd,
    own, core_send, core_recv, x_send, x_recv,
    dg, du, hid,
    part, y_send, y_recv, z_send, z_recv, mine,
    w_sem, out_sem, a_send, a_recv, c_ssem, c_rsem, x_ssem, x_rsem,
    h_ssem, h_rsem, y_ssem, y_rsem, z_ssem, z_rsem,
):
    row, col = lax.axis_index("row"), lax.axis_index("col")
    core, zy = lax.rem(row, 2), lax.rem(col, 2)
    sib = row + 1 - 2 * core
    across = lax.rem(row + 2, 4)
    y_peer = col + 1 - 2 * zy
    z = col // 2
    z_to = [None] + [lax.rem(col + 2 * d, 8) for d in (1, 2, 3)]
    z_from = [None] + [lax.rem(col + 8 - 2 * d, 8) for d in (1, 2, 3)]
    y_from = [None] + [lax.rem(y_peer + 8 - 2 * d, 8) for d in (1, 2, 3)]

    w_copies = [
        pltpu.make_async_copy(src, dst, w_sem.at[k])
        for k, (src, dst) in enumerate(((wg_hbm, wg), (wu_hbm, wu), (wd_hbm, wd)))
    ]
    for copy in w_copies:
        copy.start()

    barrier = pltpu.get_barrier_semaphore()
    for peer in ((sib, col), (across, col), (row, y_peer),
                 (row, z_to[1]), (row, z_to[2]), (row, z_to[3])):
        pl.semaphore_signal(barrier, inc=1, device_id=peer, device_id_type=MESH)
    pl.semaphore_wait(barrier, 6)

    def send(src, dst, ssem, rsem, peer):
        return pltpu.make_async_remote_copy(
            src_ref=src, dst_ref=dst, send_sem=ssem, recv_sem=rsem,
            device_id=peer, device_id_type=MESH,
        )

    n = tok_ref.shape[0]

    def block(index):
        return pl.ds(pl.multiple_of(index * n, n), n)

    gathers = ((tok_ref, tok_all), (cot_ref, cot_all))
    sends = []

    def spread(a):
        src, dst = gathers[a]
        for k, peer in ((2, z_to[2]), (1, z_to[1]), (3, z_to[3]), (0, y_peer)):
            sends.append(send(src, dst.at[block(col)], a_send.at[a, k], a_recv.at[a, k], (row, peer)))
            sends[-1].start()
        dst[block(col), :] = src[...]

    def arrived(a, k, source):
        dst = gathers[a][1].at[block(source)]
        send(dst, dst, a_send.at[a, k], a_recv.at[a, k], (row, y_peer)).wait_recv()

    def relay(a):
        dst = gathers[a][1]
        for d in (1, 3, 2):
            arrived(a, d, z_from[d])
            there = dst.at[block(z_from[d])]
            sends.append(send(there, there, a_send.at[a, 3 + d], a_recv.at[a, 3 + d], (row, y_peer)))
            sends[-1].start()

    def complete(a):
        arrived(a, 0, y_peer)
        for d in (1, 3, 2):
            arrived(a, 3 + d, y_from[d])

    width = wg.shape[1]
    half = tok_all.shape[0] // 2
    mine_rows = pl.ds(pl.multiple_of(core * half, half), half)

    def split(m, at, full):
        low, high = full[:half], full[half:]
        first = core == 0
        own[m, :, at] = jnp.where(first, low, high)
        core_send[m, :, at] = jnp.where(first, high, low)

    def forward(m, run):
        @pl.loop(run.start // TILE, (run.start + run.size) // TILE)
        def _(t):
            at = pl.ds(pl.multiple_of(t * TILE, TILE), TILE)
            if m == 2:
                full = contract_last(cot_all[...], wd[at, :])
            else:
                full = jnp.dot(tok_all[...], (wg, wu)[m][:, at], preferred_element_type=F32)
            split(m, at, full)

    first = -(-(width // TILE) // 2) * TILE
    runs = [(m, k, pl.ds(at, size)) for m in range(3) for k, (at, size) in enumerate(((0, first), (first, width - first)))]
    c_copies = [send(core_send.at[m, :, at], core_recv.at[m, :, at], c_ssem.at[m, k], c_rsem.at[m, k], (sib, col)) for m, k, at in runs]
    x_copies = [send(x_send.at[m, :, at], x_recv.at[m, :, at], x_ssem.at[m, k], x_rsem.at[m, k], (across, col)) for m, k, at in runs]

    def over_chip(i):
        m, _, run = runs[i]
        c_copies[i].wait_recv()

        @pl.loop(run.start // TILE, (run.start + run.size) // TILE)
        def _(t):
            at = pl.ds(pl.multiple_of(t * TILE, TILE), TILE)
            total = own[m, :, at] + core_recv[m, :, at]
            own[m, :, at] = total
            x_send[m, :, at] = total.astype(BF16)
        x_copies[i].start()

    spread(0)
    relay(0)
    spread(1)
    complete(0)
    for i, (m, k, run) in enumerate(runs):
        if k == 0:
            if m == 2:
                over_chip(i - 1)
                complete(1)
            w_copies[m].wait()
        forward(m, run)
        c_copies[i].start()
        if i > 0 and not (m == 2 and k == 0):
            over_chip(i - 1)
        if i == RELAY:
            relay(1)
    over_chip(len(runs) - 1)

    outs = [
        pltpu.make_async_copy(src, dst, out_sem.at[k])
        for k, (src, dst) in enumerate(
            ((tok_all, tok_out), (cot_all, cot_out), (dg, dg_out), (du, du_out), (hid, hid_out)))
    ]
    outs[0].start()
    outs[1].start()

    for copy in x_copies:
        copy.wait_recv()

    @pl.loop(0, width // TILE)
    def _(t):
        at = pl.ds(pl.multiple_of(t * TILE, TILE), TILE)
        gate, up, grad_hidden = (own[m, :, at] + x_recv[m, :, at].astype(F32) for m in range(3))
        sig = jax.nn.sigmoid(gate)
        act = gate * sig
        hid[mine_rows, at] = (act * up).astype(BF16)
        du[mine_rows, at] = (grad_hidden * act).astype(BF16)
        dg[mine_rows, at] = (grad_hidden * up * sig * (1.0 + gate * (1.0 - sig))).astype(BF16)

    h_copies = [
        send(ref.at[mine_rows], ref.at[mine_rows], h_ssem.at[k], h_rsem.at[k], (sib, col))
        for k, ref in enumerate((dg, du, hid))
    ]
    for copy in h_copies:
        copy.start()
    their_rows = pl.ds(pl.multiple_of((1 - core) * half, half), half)
    for k, ref in enumerate((dg, du, hid)):
        there = ref.at[their_rows]
        send(there, there, h_ssem.at[k], h_rsem.at[k], (sib, col)).wait_recv()
    for k in (2, 3, 4):
        outs[k].start()

    span = wg.shape[0] // GROUPS
    y_copies = [send(y_send.at[g], y_recv.at[g], y_ssem.at[g], y_rsem.at[g], (row, y_peer)) for g in range(GROUPS)]
    z_copies = [
        [send(z_send.at[g, d - 1], z_recv.at[g, d - 1], z_ssem.at[g, d - 1], z_rsem.at[g, d - 1], (row, z_to[d]))
         for d in (1, 2, 3)]
        for g in range(GROUPS)
    ]

    def backward(g):
        @pl.loop(0, span // TILE)
        def _(t):
            at = pl.ds(pl.multiple_of(t * TILE, TILE), TILE)
            rows = pl.ds(pl.multiple_of(g * span + t * TILE, TILE), TILE)
            full = contract_last(dg[...], wg[rows, :]) + contract_last(du[...], wu[rows, :])
            part[g, :, :, at] = full.reshape(8, n, TILE)
        for k in range(4):
            y_send[g, k] = part[g, y_peer - 2 * z + 2 * k].astype(BF16)
        y_copies[g].start()

    def along_z(g):
        y_copies[g].wait_recv()
        for d in (1, 2, 3):
            to = lax.rem(z + d, 4)
            z_send[g, d - 1] = (part[g, 2 * to + zy] + y_recv[g, to].astype(F32)).astype(BF16)
            z_copies[g][d - 1].start()
        mine[g] = part[g, col] + y_recv[g, z].astype(F32)

    for g in range(GROUPS):
        backward(g)
        if g > 0:
            along_z(g - 1)
    along_z(GROUPS - 1)
    for g in range(GROUPS):
        total = mine[g]
        for d in (1, 2, 3):
            z_copies[g][d - 1].wait_recv()
            total = total + z_recv[g, d - 1].astype(F32)
        gt_ref[:, g * span:(g + 1) * span] = total.astype(BF16)

    for copy in sends + c_copies + x_copies + h_copies + y_copies:
        copy.wait_send()
    for group in z_copies:
        for copy in group:
            copy.wait_send()
    for copy in outs:
        copy.wait()


def main(tokens, cotangent, gate_weight, up_weight, down_weight):
    n, depth = tokens.shape
    width = gate_weight.shape[1]
    all_tokens = 8 * n
    half = all_tokens // 2
    span = depth // GROUPS
    hbm, vmem = pl.BlockSpec(memory_space=pl.ANY), pl.BlockSpec(memory_space=pltpu.VMEM)
    dma = pltpu.SemaphoreType.DMA
    return pl.pallas_call(
        main_kernel,
        out_shape=(
            jax.ShapeDtypeStruct((n, depth), BF16),
            jax.ShapeDtypeStruct((all_tokens, depth), BF16),
            jax.ShapeDtypeStruct((all_tokens, depth), BF16),
            jax.ShapeDtypeStruct((all_tokens, width), BF16),
            jax.ShapeDtypeStruct((all_tokens, width), BF16),
            jax.ShapeDtypeStruct((all_tokens, width), BF16),
        ),
        in_specs=[vmem, vmem, hbm, hbm, hbm],
        out_specs=(vmem, hbm, hbm, hbm, hbm, hbm),
        scratch_shapes=[
            pltpu.VMEM((all_tokens, depth), BF16),
            pltpu.VMEM((all_tokens, depth), BF16),
            pltpu.VMEM((depth, width), BF16),
            pltpu.VMEM((depth, width), BF16),
            pltpu.VMEM((width, depth), BF16),
            pltpu.VMEM((3, half, width), F32),
            pltpu.VMEM((3, half, width), F32),
            pltpu.VMEM((3, half, width), F32),
            pltpu.VMEM((3, half, width), BF16),
            pltpu.VMEM((3, half, width), BF16),
            pltpu.VMEM((all_tokens, width), BF16),
            pltpu.VMEM((all_tokens, width), BF16),
            pltpu.VMEM((all_tokens, width), BF16),
            pltpu.VMEM((GROUPS, 8, n, span), F32),
            pltpu.VMEM((GROUPS, 4, n, span), BF16),
            pltpu.VMEM((GROUPS, 4, n, span), BF16),
            pltpu.VMEM((GROUPS, 3, n, span), BF16),
            pltpu.VMEM((GROUPS, 3, n, span), BF16),
            pltpu.VMEM((GROUPS, n, span), F32),
            dma((3,)), dma((5,)), dma((2, 7)), dma((2, 7)),
            dma((3, 2)), dma((3, 2)), dma((3, 2)), dma((3, 2)),
            dma((3,)), dma((3,)), dma((GROUPS,)), dma((GROUPS,)),
            dma((GROUPS, 3)), dma((GROUPS, 3)),
        ],
        compiler_params=pltpu.CompilerParams(
            collective_id=0, has_side_effects=True, vmem_limit_bytes=56 * 1024 * 1024
        ),
    )(tokens, cotangent, gate_weight, up_weight, down_weight)


def weight_kernel(tok_ref, dg_ref, du_ref, hid_ref, cot_ref, gg_ref, gu_ref, gd_ref, turned):
    @pl.when(pl.program_id(0) == 0)
    def _():
        turned[...] = tok_ref[...].T

    tok = turned[...]
    gg_ref[...] = jnp.dot(tok, dg_ref[...], preferred_element_type=F32).astype(BF16)
    gu_ref[...] = jnp.dot(tok, du_ref[...], preferred_element_type=F32).astype(BF16)
    gd_ref[...] = contract_first(hid_ref[...], cot_ref[...]).astype(BF16)


def weight_grads(tok_all, dg, du, hid, cot_all):
    rows, depth = tok_all.shape
    width = dg.shape[1]

    def whole(array):
        return pl.BlockSpec(array.shape, lambda i: (0, 0))

    tile = pl.BlockSpec((rows, TILE), lambda i: (0, i))
    return pl.pallas_call(
        weight_kernel,
        grid=(width // TILE,),
        out_shape=(
            jax.ShapeDtypeStruct((depth, width), BF16),
            jax.ShapeDtypeStruct((depth, width), BF16),
            jax.ShapeDtypeStruct((width, depth), BF16),
        ),
        in_specs=[whole(tok_all), tile, tile, tile, whole(cot_all)],
        out_specs=(
            pl.BlockSpec((depth, TILE), lambda i: (0, i)),
            pl.BlockSpec((depth, TILE), lambda i: (0, i)),
            pl.BlockSpec((TILE, depth), lambda i: (i, 0)),
        ),
        scratch_shapes=[pltpu.VMEM((depth, rows), BF16)],
        compiler_params=pltpu.CompilerParams(vmem_limit_bytes=62 * 1024 * 1024),
    )(tok_all, dg, du, hid, cot_all)


def local(tokens, cotangent, gate_weight, up_weight, down_weight):
    grad_tokens, tok_all, cot_all, dg, du, hid = main(
        tokens, cotangent, gate_weight, up_weight, down_weight
    )
    grad_gate, grad_up, grad_down = weight_grads(tok_all, dg, du, hid, cot_all)
    return (grad_tokens, grad_gate, grad_up, grad_down)


def gating(gate, up, grad_hidden):
    sig = jax.nn.sigmoid(gate)
    act = gate * sig
    hidden = (act * up).astype(BF16)
    d_up = (grad_hidden * act).astype(BF16)
    d_gate = (grad_hidden * up * sig * (1.0 + gate * (1.0 - sig))).astype(BF16)
    return d_gate, d_up, hidden


def local_any(tokens, cotangent, gate_weight, up_weight, down_weight):
    def gather(array, axis):
        return lax.all_gather(array, axis, axis=0, tiled=True)

    def scatter(array, axis):
        return lax.psum_scatter(array, axis, scatter_dimension=0, tiled=True)

    tok_all, cot_all = gather(tokens, "col"), gather(cotangent, "col")
    gate = scatter(jnp.dot(tok_all, gate_weight, preferred_element_type=F32), "row")
    up = scatter(jnp.dot(tok_all, up_weight, preferred_element_type=F32), "row")
    grad_hidden = scatter(contract_last(cot_all, down_weight), "row")
    dg, du, hid = (gather(part, "row") for part in gating(gate, up, grad_hidden))
    grad_tokens = scatter(
        contract_last(dg, gate_weight) + contract_last(du, up_weight), "col"
    ).astype(BF16)
    return (
        grad_tokens,
        contract_first(tok_all, dg).astype(BF16),
        contract_first(tok_all, du).astype(BF16),
        contract_first(hid, cot_all).astype(BF16),
    )


def solution(mesh):
    fits = mesh.shape["row"] == 4 and mesh.shape["col"] == 8
    return jax.shard_map(
        local if fits else local_any,
        mesh=mesh,
        in_specs=(
            P("col", "row"),
            P("col", "row"),
            P("row", "col"),
            P("row", "col"),
            P("col", "row"),
        ),
        out_specs=(P("col", "row"), P("row", "col"), P("row", "col"), P("col", "row")),
        check_vma=False,
    )
```
